32 devices in a mesh: gx: 4 (over x, core), gy: 2 (over y), gz: 4 (over z).
Axes of the slice: x: 2, y: 2, z: 4, core: 2. Of those that a mesh axis runs over, the one named last changes fastest.
Arguments:
- right_side: float32 [128, 32, 512], P('gx', 'gy', 'gz'), may hold values from -6 to 6
- phase_label: int32 [128, 32, 512], P('gx', 'gy', 'gz'), may hold values from 0 to 2
- viscosity: float32 [128, 32, 512], P('gx', 'gy', 'gz'), may hold values from 0.5 to 4
- mobility_table: float32 [3], replicated, may hold values from 0.05 to 2
- shift_table: float32 [3], replicated, may hold values from 0.0005 to 0.004
Outputs:
- correction: float32 [128, 32, 512], P('gx', 'gy', 'gz')
The draws below stay inside these ranges and needn't reach their ends.
All inputs are finite; a program needn't handle non-finite values.
Results may differ from the reference program's by a relative error of at most 0.00002.
Values sent between devices are 32-bit elements; how exact they have to be, the bound alone decides.
A program may use at most 128 MiB of HBM per device.

```python
import math
import jax
import jax.numpy as jnp
from jax import lax

LEVELS = 5
COARSE_SWEEPS = 48
PHASES = 3
NX = 128
NY = 32
NZ = 512


def with_ends(result, rng, least, top_value):
    longest = result.shape.index(max(result.shape))
    spots = []
    for shift in (0, 1):
        where = [jax.random.randint(jax.random.fold_in(rng, axis), (), 0, length) for axis, length in enumerate(result.shape)]
        where[longest] = (where[longest] + shift) % result.shape[longest]
        spots.append(tuple(where))
    return result.at[spots[0]].set(least).at[spots[1]].set(top_value)


def shard_levels(rng, dims, shards, least, top_value):
    def one(axis_at, shards_of):
        draws = jax.random.uniform(jax.random.fold_in(jax.random.fold_in(rng, 6), axis_at), (shards_of,), jnp.float32, least / len(shards), top_value / len(shards))
        return jnp.repeat(jnp.exp(draws), dims[axis_at] // shards_of).reshape((-1,) + (1,) * (len(dims) - axis_at - 1))

    gain = one(*shards[0])
    for cut in shards[1:]:
        gain = gain * one(*cut)
    return gain


def centred(stream_key, dims, scale, bound, pieces=(), held_as=jnp.bfloat16):
    array = jax.random.normal(stream_key, dims, jnp.float32) * scale
    if len(pieces) > 0:
        array = shard_levels(stream_key, dims, pieces, -0.22, 0.18) * array
    return jnp.clip(array, min=-bound, max=bound).astype(held_as)


def setup_inputs(seed: int = 0) -> dict:
    keys = jax.random.split(jax.random.key(seed), 6)
    return {
        "right_side": centred(keys[0], (NX, NY, NZ), 1.0, 6.0, ((0, 4), (1, 2), (2, 4)), jnp.float32),
        "phase_label": with_ends(jax.random.randint(keys[1], (NX, NY, NZ), 0, PHASES), jax.random.fold_in(keys[1], 1), 0, PHASES - 1).astype(jnp.int32),
        "viscosity": jnp.clip(jnp.exp(math.log(4.0) - 2.0794415 * jax.random.uniform(keys[2], (NX, NY, NZ), jnp.float32) ** shard_levels(keys[2], (NX, NY, NZ), ((0, 4), (1, 2), (2, 4)), -0.2, 0.2)), 0.5, 4.0),
        "mobility_table": jnp.clip(jnp.exp(jax.random.uniform(keys[3], (PHASES,), jnp.float32, math.log(0.05), math.log(2.0))), 0.05, 2.0),
        "shift_table": jnp.clip(jnp.exp(jax.random.uniform(keys[4], (PHASES,), jnp.float32, math.log(0.0005), math.log(0.004))), 0.0005, 0.004),
    }


OMEGA = 0.8


def harmonic(first, second):
    return 2.0 * first * second / (first + second)


def neighbours(padded):
    return [padded[2:, 1:-1, 1:-1], padded[:-2, 1:-1, 1:-1],
            padded[1:-1, 2:, 1:-1], padded[1:-1, :-2, 1:-1],
            padded[1:-1, 1:-1, 2:], padded[1:-1, 1:-1, :-2]]


def face_terms(padded, mobility):
    return [harmonic(mobility, other) for other in neighbours(padded)]


def operate(padded, field, terms, shift):
    total = shift * field
    for term, other in zip(terms, neighbours(padded)):
        total = total + term * (field - other)
    return total


def diagonal_of(terms, shift):
    total = shift
    for term in terms:
        total = total + term
    return total


def block_sum(field):
    a, b, c = field.shape
    return field.reshape(a // 2, 2, b // 2, 2, c // 2, 2).sum(axis=(1, 3, 5))


def spread(field):
    return jnp.repeat(jnp.repeat(jnp.repeat(field, 2, 0), 2, 1), 2, 2)


def coarse_solve(rhs, mobility, shift):
    terms = face_terms(jnp.pad(mobility, 1), mobility)
    diag = diagonal_of(terms, shift)
    start = OMEGA * rhs / diag

    def sweep(step, field):
        return field + OMEGA * (rhs - operate(jnp.pad(field, 1), field, terms, shift)) / diag

    return lax.fori_loop(0, COARSE_SWEEPS - 1, sweep, start)


def cycle(level, rhs, mobility, shift):
    if level == LEVELS - 1:
        return coarse_solve(rhs, mobility, shift)
    terms = face_terms(jnp.pad(mobility, 1), mobility)
    diag = diagonal_of(terms, shift)
    field = OMEGA * rhs / diag
    field = field + OMEGA * (rhs - operate(jnp.pad(field, 1), field, terms, shift)) / diag
    remain = rhs - operate(jnp.pad(field, 1), field, terms, shift)
    coarse = cycle(level + 1, block_sum(remain), block_sum(mobility) / 4.0, block_sum(shift))
    field = field + spread(coarse)
    for sweep_index in range(2):
        field = field + OMEGA * (rhs - operate(jnp.pad(field, 1), field, terms, shift)) / diag
    return field


def reference(right_side, phase_label, viscosity, mobility_table, shift_table):
    mobility = mobility_table[phase_label] / viscosity
    shift = shift_table[phase_label]
    return cycle(0, right_side, mobility, shift)
```

```python
import functools
import jax
import jax.numpy as jnp
from jax import lax
from jax.sharding import PartitionSpec as P
from jax.experimental import pallas as pl
from jax.experimental.pallas import tpu as pltpu

LEVELS = 5
COARSE_SWEEPS = 48
OMEGA = 0.8
LANES = 128
CHUNK = 8
MESH = pl.DeviceIdType.MESH


def dot(a, b):
    return jnp.dot(a, b, precision=lax.Precision.HIGHEST, preferred_element_type=jnp.float32)


def iota(shape, dim):
    return lax.broadcasted_iota(jnp.int32, shape, dim)


def ones_where(mask):
    return jnp.where(mask, 1.0, 0.0).astype(jnp.float32)


def pair_lanes(fine, coarse, zf, zc):
    i, j = iota((fine, coarse), 0), iota((fine, coarse), 1)
    return ones_where(((i // zf) // 2 == j // zc) & ((i % zf) // 2 == j % zc))


def pair_lanes_back(coarse, fine, zf, zc):
    j, i = iota((coarse, fine), 0), iota((coarse, fine), 1)
    return ones_where(((i // zf) // 2 == j // zc) & ((i % zf) // 2 == j % zc))


def kernel(sizes, b_ref, ph_ref, visc_ref, mt_ref, st_ref, out_ref,
           xa0, xb0, w0, inv0, dg0, zh0, sy0, sz0, rx0, ry0, rz0,
           xa1, xb1, w1, inv1, dg1, zh1, sy1, sz1, rx1, ry1, rz1,
           s0, base0, base1, r0, r1, m1, s1, t256, t128, t64,
           pk_ms, pk_r, g_ms, g_r, x2, wj2, wj3, dj2, dj3,
           ss, rs, gsem):
    GX, GY, GZ = sizes
    N = GX * GY * GZ
    ix, iy, iz = lax.axis_index("gx"), lax.axis_index("gy"), lax.axis_index("gz")
    me = (ix * GY + iy) * GZ + iz
    axes = ((ix, GX), (iy, GY), (iz, GZ))
    L0 = dict(n=(32, 16, 128), w=w0, inv=inv0, dg=dg0, zh=zh0, sy=sy0, sz=sz0, r=(rx0, ry0, rz0), off=0, base=base0)
    L1 = dict(n=(16, 8, 64), w=w1, inv=inv1, dg=dg1, zh=zh1, sy=sy1, sz=sz1, r=(rx1, ry1, rz1), off=5, base=base1)

    def copies(L, xp, e):
        nx = L["n"][0]
        srcs = ((xp.at[1], xp.at[nx]), (L["sy"].at[0], L["sy"].at[1]), (L["sz"].at[0], L["sz"].at[1]))
        out = []
        for a in range(3):
            pos, count = axes[a]
            for side in range(2):
                to = [ix, iy, iz]
                to[a] = pos - 1 if side == 0 else pos + 1
                there = pos > 0 if side == 0 else pos < count - 1
                k = L["off"] + e
                out.append((there, pltpu.make_async_remote_copy(
                    src_ref=srcs[a][side], dst_ref=L["r"][a].at[e, 1 - side],
                    send_sem=ss.at[k, 2 * a + side], recv_sem=rs.at[k, 2 * a + 1 - side],
                    device_id=tuple(to), device_id_type=MESH), L["r"][a].at[e, side]))
        return out

    def start(L, xp, e):
        nx, ny, nz = L["n"]
        todo = copies(L, xp, e)

        def go(which):
            for there, copy, _ in which:
                @pl.when(there)
                def _(copy=copy):
                    copy.start()
        go(todo[0:2])
        for c in range(nx // CHUNK):
            v = xp[1 + c * CHUNK:1 + (c + 1) * CHUNK]
            L["sy"][0, c * CHUNK:(c + 1) * CHUNK, :] = v[:, 0, :]
            L["sy"][1, c * CHUNK:(c + 1) * CHUNK, :] = v[:, ny - 1, :]
        go(todo[2:4])
        per = LANES // ny
        for k in range(nx // per):
            t = xp[1 + k * per:1 + (k + 1) * per].reshape(LANES, LANES).T
            L["sz"][0, k:k + 1, :] = t[0:1, :]
            L["sz"][1, k:k + 1, :] = t[nz - 1:nz, :]
        go(todo[4:6])

    def finish(L, xp, e):
        nx, ny, nz = L["n"]
        todo = copies(L, xp, e)
        for a in range(3):
            for side in range(2):
                there, copy, slot = todo[2 * a + side]
                other = todo[2 * a + 1 - side][1]

                @pl.when(there)
                def _(copy=copy, other=other):
                    copy.wait_send()
                    other.wait_recv()

                @pl.when(jnp.logical_not(there))
                def _(slot=slot):
                    slot[...] = jnp.zeros(slot.shape, jnp.float32)
        rx, ry, rz = L["r"]
        xp[0] = rx[e, 0]
        xp[nx + 1] = rx[e, 1]
        per = LANES // ny
        row = iota((LANES, LANES), 0)
        for k in range(nx // per):
            low = jnp.broadcast_to(rz[e, 0, k:k + 1, :], (LANES, LANES))
            high = jnp.broadcast_to(rz[e, 1, k:k + 1, :], (LANES, LANES))
            t = jnp.where(row == 0, low, jnp.where(row == nz - 1, high, 0.0)).T
            L["zh"][k * per:(k + 1) * per] = t.reshape(per, ny, LANES)

    def around(L, xp, e, i):
        nx, ny, nz = L["n"]
        shape = (CHUNK, ny, LANES)
        ry = L["r"][1]
        at = pl.multiple_of(i * CHUNK, CHUNK)
        v = xp[pl.ds(1 + at, CHUNK)]
        zh = L["zh"][pl.ds(at, CHUNK)]
        row, lane = iota(shape, 1), iota(shape, 2)
        low = jnp.broadcast_to(ry[e, 0, pl.ds(at, CHUNK), :][:, None, :], shape)
        high = jnp.broadcast_to(ry[e, 1, pl.ds(at, CHUNK), :][:, None, :], shape)
        return v, [xp[pl.ds(2 + at, CHUNK)], xp[pl.ds(at, CHUNK)],
                   jnp.where(row == ny - 1, high, pltpu.roll(v, ny - 1, 1)),
                   jnp.where(row == 0, low, pltpu.roll(v, 1, 1)),
                   jnp.where(lane == nz - 1, zh, pltpu.roll(v, LANES - 1, 2)),
                   jnp.where(lane == 0, zh, pltpu.roll(v, 1, 2))]

    def chunks(L, fn):
        def step(i, _):
            fn(i)
            return 0
        lax.fori_loop(0, L["n"][0] // CHUNK, step, 0)

    def coefficients(L, mp, e, s_ref):
        nx, ny, nz = L["n"]

        def one(i):
            at = pl.multiple_of(i * CHUNK, CHUNK)
            m, near = around(L, mp, e, i)
            valid = iota((CHUNK, ny, LANES), 2) < nz
            diag = s_ref[pl.ds(at, CHUNK)]
            terms = []
            for n in near:
                t = 2.0 * m * n / (m + n)
                if nz < LANES:
                    t = jnp.where(valid, t, 0.0)
                diag = diag + t
                terms.append(t)
            if nz < LANES:
                diag = jnp.where(valid, diag, 1.0)
            inv = OMEGA / diag
            L["inv"][pl.ds(at, CHUNK)] = inv
            L["dg"][pl.ds(at, CHUNK)] = diag * (1.0 / OMEGA)
            for d in range(6):
                L["w"][d, pl.ds(at, CHUNK)] = terms[d] * inv
        chunks(L, one)

    def begin(L, rhs, xp):
        def one(i):
            at = pl.multiple_of(i * CHUNK, CHUNK)
            v = rhs[pl.ds(at, CHUNK)] * L["inv"][pl.ds(at, CHUNK)]
            L["base"][pl.ds(at, CHUNK)] = v
            xp[pl.ds(1 + at, CHUNK)] = v
        chunks(L, one)

    def sweep(L, xp, e, put):
        def one(i):
            at = pl.multiple_of(i * CHUNK, CHUNK)
            v, near = around(L, xp, e, i)
            total = (1.0 - OMEGA) * v + L["base"][pl.ds(at, CHUNK)]
            for d in range(6):
                total = total + L["w"][d, pl.ds(at, CHUNK)] * near[d]
            put(at, v, total)
        chunks(L, one)

    def into(xp):
        def put(at, v, total):
            xp[pl.ds(1 + at, CHUNK)] = total
        return put

    def residual(L, r):
        def put(at, v, total):
            r[pl.ds(at, CHUNK)] = L["dg"][pl.ds(at, CHUNK)] * (total - v)
        return put

    def restrict0(load):
        halve = pair_lanes(LANES, LANES, LANES, 64)
        for c in range(2):
            v = load(c).reshape(8, 2, 16, LANES)
            v = v[:, 0] + v[:, 1]
            t256[c * 128:(c + 1) * 128, :] = dot(v.reshape(128, LANES), halve)
        return (t256[pl.ds(0, 128, stride=2), :] + t256[pl.ds(1, 128, stride=2), :]).reshape(16, 8, LANES)

    def pack(v):
        v = v.reshape(8, 2, 8, LANES)
        t64[...] = (v[:, 0] + v[:, 1]).reshape(64, LANES)
        total = jnp.zeros((8, LANES), jnp.float32)
        i, j = iota((LANES, LANES), 0), iota((LANES, LANES), 1)
        for q in range(4):
            place = ones_where((i < 64) & (j == 32 * q + i // 2))
            both = t64[pl.ds(2 * q, 8, stride=8), :] + t64[pl.ds(2 * q + 1, 8, stride=8), :]
            total = total + dot(both, place)
        return total

    def gather_start(src, dst, k):
        def send(step, _):
            peer = lax.rem(me + step, N)
            to = (peer // (GY * GZ), lax.rem(peer // GZ, GY), lax.rem(peer, GZ))
            pltpu.make_async_remote_copy(
                src_ref=src, dst_ref=dst.at[me], send_sem=gsem.at[2 * k], recv_sem=gsem.at[2 * k + 1],
                device_id=to, device_id_type=MESH).start()
            return 0
        lax.fori_loop(1, N, send, 0)

    def gather_finish(src, dst, k):
        rest = dst.at[pl.ds(0, N - 1)]
        pltpu.make_async_copy(rest, rest, gsem.at[2 * k]).wait()
        pltpu.make_async_copy(rest, rest, gsem.at[2 * k + 1]).wait()
        dst[pl.ds(me, 1)] = src[...][None]

    X2, Y2, Z2 = 8 * GX, 4 * GY, 32 * GZ

    def unpack(read):
        lane = iota((8, LANES), 1)
        rows = []
        for gx in range(GX):
            tiles = []
            for y in range(Y2):
                gy, q = y // 4, y % 4
                for t in range(Z2 // LANES):
                    tile = jnp.zeros((8, LANES), jnp.float32)
                    for p in range(4):
                        v = read((gx * GY + gy) * GZ + 4 * t + p)
                        shift = (32 * (p - q)) % LANES
                        v = pltpu.roll(v, shift, 1) if shift else v
                        tile = jnp.where(lane // 32 == p, v, tile)
                    tiles.append(tile)
            rows.append(jnp.concatenate(tiles, axis=1))
        return jnp.concatenate(rows, axis=0)

    def flat_terms(m, s, dims):
        X, Y, Z = dims
        shape = m.shape
        row, lane = iota(shape, 0), iota(shape, 1)
        width = shape[1]
        valid = lane < Y * Z
        z, y = lane % Z, lane // Z
        inside = [row < X - 1, row > 0, y < Y - 1, y > 0, z < Z - 1, z > 0]
        diag = s
        terms = []
        for near, ok in zip(flat_near(m, Z), inside):
            t = jnp.where(ok & valid, 2.0 * m * near / (m + near), 0.0)
            diag = diag + t
            terms.append(t)
        diag = jnp.where(valid, diag, 1.0)
        inv = OMEGA / diag
        return [t * inv for t in terms], inv, diag * (1.0 / OMEGA)

    def flat_near(v, Z):
        X, width = v.shape
        return [pltpu.roll(v, X - 1, 0), pltpu.roll(v, 1, 0),
                pltpu.roll(v, width - Z, 1), pltpu.roll(v, Z, 1),
                pltpu.roll(v, width - 1, 1), pltpu.roll(v, 1, 1)]

    def flat_sweep(v, base, w, Z):
        total = (1.0 - OMEGA) * v + base
        for d, near in enumerate(flat_near(v, Z)):
            total = total + w[d] * near
        return total

    def flat_restrict(r, dims):
        X, Y, Z = dims
        span = min(4 * LANES, Y * Z)
        place = pair_lanes(span, LANES, Z, Z // 2)
        tiles = [dot(r[:, k * span:(k + 1) * span], place) for k in range(Y * Z // span)]
        wide = jnp.concatenate(tiles, axis=1) if len(tiles) > 1 else tiles[0]
        left = ones_where(iota((X // 2, X), 1) // 2 == iota((X // 2, X), 0))
        return dot(left, wide)

    def flat_spread(e, dims):
        X, Y, Z = dims
        span = min(4 * LANES, Y * Z)
        left = ones_where(iota((X, X // 2), 0) // 2 == iota((X, X // 2), 1))
        tall = dot(left, e)
        place = pair_lanes_back(LANES, span, Z, Z // 2)
        tiles = [dot(tall[:, k * LANES:(k + 1) * LANES], place) for k in range(Y * Z // span)]
        return jnp.concatenate(tiles, axis=1) if len(tiles) > 1 else tiles[0]

    d2 = (X2, Y2, Z2)
    d3 = (X2 // 2, Y2 // 2, Z2 // 2)
    d4 = (X2 // 4, Y2 // 4, Z2 // 4)

    sz0[...] = jnp.zeros(sz0.shape, jnp.float32)
    sz1[...] = jnp.zeros(sz1.shape, jnp.float32)

    def look_up(i):
        at = pl.multiple_of(i * CHUNK, CHUNK)
        ph = ph_ref[pl.ds(at, CHUNK)]
        mob = jnp.full(ph.shape, mt_ref[0], jnp.float32)
        shift = jnp.full(ph.shape, st_ref[0], jnp.float32)
        for k in range(1, mt_ref.shape[0]):
            mob = jnp.where(ph == k, mt_ref[k], mob)
            shift = jnp.where(ph == k, st_ref[k], shift)
        xb0[pl.ds(1 + at, CHUNK)] = mob / visc_ref[pl.ds(at, CHUNK)]
        s0[pl.ds(at, CHUNK)] = shift
    chunks(L0, look_up)
    start(L0, xb0, 0)

    lane1 = iota((16, 8, LANES), 2)
    mob1 = restrict0(lambda c: xb0[1 + 16 * c:17 + 16 * c]) * 0.25
    xb1[1:17] = jnp.where(lane1 < 64, mob1, 1.0)
    start(L1, xb1, 0)
    s1[...] = restrict0(lambda c: s0[16 * c:16 + 16 * c])
    pk_ms[0:8, :] = pack(mob1) * 0.25
    pk_ms[8:16, :] = pack(s1[...])
    gather_start(pk_ms, g_ms, 0)

    finish(L0, xb0, 0)
    coefficients(L0, xb0, 0, s0)
    begin(L0, b_ref, xa0)
    start(L0, xa0, 1)
    finish(L1, xb1, 0)
    coefficients(L1, xb1, 0, s1)
    finish(L0, xa0, 1)
    sweep(L0, xa0, 1, into(xb0))
    start(L0, xb0, 2)

    gather_finish(pk_ms, g_ms, 0)
    m2 = unpack(lambda n: g_ms[n, 0:8, :])
    s2 = unpack(lambda n: g_ms[n, 8:16, :])
    w, inv, dg = flat_terms(m2, s2, d2)
    for d in range(6):
        wj2[d] = w[d]
    dj2[0], dj2[1] = inv, dg
    m3 = flat_restrict(m2, d2) * 0.25
    s3 = flat_restrict(s2, d2)
    w, inv, dg = flat_terms(m3, s3, d3)
    for d in range(6):
        wj3[d] = w[d]
    dj3[0], dj3[1] = inv, dg
    m4 = flat_restrict(m3, d3) * 0.25
    s4 = flat_restrict(s3, d3)
    w4, inv4, _ = flat_terms(m4, s4, d4)

    finish(L0, xb0, 2)
    sweep(L0, xb0, 2, residual(L0, r0))
    r1[...] = restrict0(lambda c: r0[16 * c:16 + 16 * c])
    begin(L1, r1, xa1)
    start(L1, xa1, 1)
    finish(L1, xa1, 1)
    sweep(L1, xa1, 1, into(xb1))
    start(L1, xb1, 2)
    finish(L1, xb1, 2)
    sweep(L1, xb1, 2, residual(L1, r1))
    pk_r[...] = pack(r1[...])
    gather_start(pk_r, g_r, 1)
    gather_finish(pk_r, g_r, 1)

    base2 = unpack(lambda n: g_r[n]) * dj2[0]
    w2 = [wj2.at[d] for d in range(6)]
    w3 = [wj3.at[d] for d in range(6)]

    def run(v, base, w, Z):
        return flat_sweep(v, base, [ref[...] for ref in w], Z)

    v2 = run(base2, base2, w2, Z2)
    b3 = flat_restrict(dj2[1] * (run(v2, base2, w2, Z2) - v2), d2)
    base3 = b3 * dj3[0]
    v3 = run(base3, base3, w3, Z2 // 2)
    b4 = flat_restrict(dj3[1] * (run(v3, base3, w3, Z2 // 2) - v3), d3)
    base4 = b4 * inv4
    v4 = lax.fori_loop(0, COARSE_SWEEPS - 1, lambda _, v: flat_sweep(v, base4, w4, Z2 // 4), base4)
    v3 = v3 + flat_spread(v4, d3)
    for _ in range(2):
        v3 = run(v3, base3, w3, Z2 // 2)
    v2 = v2 + flat_spread(v3, d2)
    for _ in range(2):
        v2 = run(v2, base2, w2, Z2)
    x2[...] = v2

    widen32 = ones_where((iota((LANES, LANES), 1) // 2 == iota((LANES, LANES), 0)) & (iota((LANES, LANES), 1) < 64))
    for q in range(4):
        column = pl.multiple_of((iy * 4 + q) * Z2 + (iz // 4) * LANES, LANES)
        tile = x2[pl.ds(pl.multiple_of(ix * 8, 8), 8), pl.ds(column, LANES)]
        tile = pltpu.roll(tile, lax.rem(LANES - 32 * lax.rem(iz, 4), LANES), 1)
        tile = dot(tile, widen32)
        t64[pl.ds(2 * q, 8, stride=8), :] = tile
        t64[pl.ds(2 * q + 1, 8, stride=8), :] = tile
    e1 = jnp.broadcast_to(t64[...].reshape(8, 1, 8, LANES), (8, 2, 8, LANES)).reshape(16, 8, LANES)
    xa1[1:17] = xb1[1:17] + e1
    start(L1, xa1, 3)
    finish(L1, xa1, 3)
    sweep(L1, xa1, 3, into(xb1))
    start(L1, xb1, 4)
    finish(L1, xb1, 4)
    sweep(L1, xb1, 4, into(xa1))

    widen64 = pair_lanes_back(LANES, LANES, LANES, 64)
    wide = dot(xa1[1:17].reshape(128, LANES), widen64)
    t256[pl.ds(0, 128, stride=2), :] = wide
    t256[pl.ds(1, 128, stride=2), :] = wide
    for c in range(16):
        e0 = t256[16 * c:16 * c + 16, :]
        xa0[1 + 2 * c] = xb0[1 + 2 * c] + e0
        xa0[2 + 2 * c] = xb0[2 + 2 * c] + e0
    start(L0, xa0, 3)
    finish(L0, xa0, 3)
    sweep(L0, xa0, 3, into(xb0))
    start(L0, xb0, 4)
    finish(L0, xb0, 4)

    def put(at, v, total):
        out_ref[pl.ds(at, CHUNK)] = total
    sweep(L0, xb0, 4, put)


def body(sizes, right_side, phase_label, viscosity, mobility_table, shift_table):
    GX, GY, GZ = sizes
    N = GX * GY * GZ
    f32 = jnp.float32
    V = lambda *shape: pltpu.VMEM(shape, f32)

    def level(nx, ny):
        return [V(nx + 2, ny, 128), V(nx + 2, ny, 128), V(6, nx, ny, 128), V(nx, ny, 128), V(nx, ny, 128), V(nx, ny, 128),
                V(2, nx, 128), V(2, 8, 128), V(5, 2, ny, 128), V(5, 2, nx, 128), V(5, 2, 8, 128)]

    X2, F2 = 8 * GX, 128 * GY * GZ
    X3, F3 = 4 * GX, max(128, 32 * GY * GZ)
    scratch = level(32, 16) + level(16, 8) + [
        V(32, 16, 128), V(32, 16, 128), V(16, 8, 128), V(32, 16, 128), V(16, 8, 128), V(16, 8, 128), V(16, 8, 128),
        V(256, 128), V(128, 128), V(64, 128),
        V(16, 128), V(8, 128), V(N, 16, 128), V(N, 8, 128),
        V(X2, F2), V(6, X2, F2), V(6, X3, F3), V(2, X2, F2), V(2, X3, F3),
        pltpu.SemaphoreType.DMA((10, 6)), pltpu.SemaphoreType.DMA((10, 6)), pltpu.SemaphoreType.DMA((4,))]
    vmem = pl.BlockSpec(memory_space=pltpu.VMEM)
    smem = pl.BlockSpec(memory_space=pltpu.SMEM)
    return pl.pallas_call(
        functools.partial(kernel, sizes),
        out_shape=jax.ShapeDtypeStruct(right_side.shape, f32),
        in_specs=[vmem, vmem, vmem, smem, smem],
        out_specs=vmem,
        scratch_shapes=scratch,
        compiler_params=pltpu.CompilerParams(has_side_effects=True, vmem_limit_bytes=56 * 2**20),
    )(right_side, phase_label, viscosity, mobility_table, shift_table)


def solution(mesh):
    sizes = tuple(mesh.shape[a] for a in ("gx", "gy", "gz"))
    in_specs = (P("gx", "gy", "gz"), P("gx", "gy", "gz"), P("gx", "gy", "gz"), P(), P())
    return jax.shard_map(functools.partial(body, sizes), mesh=mesh, in_specs=in_specs,
                         out_specs=P("gx", "gy", "gz"), check_vma=False)
```

```python
import functools
import jax
import jax.numpy as jnp
from jax import lax
from jax.sharding import PartitionSpec as P
from jax.experimental import pallas as pl
from jax.experimental.pallas import tpu as pltpu

LEVELS = 5
COARSE_SWEEPS = 48
OMEGA = 0.8
LANES = 128
CHUNK = 8
MESH = pl.DeviceIdType.MESH


def dot(a, b):
    return jnp.dot(a, b, precision=lax.Precision.HIGHEST, preferred_element_type=jnp.float32)


def iota(shape, dim):
    return lax.broadcasted_iota(jnp.int32, shape, dim)


def ones_where(mask):
    return jnp.where(mask, 1.0, 0.0).astype(jnp.float32)


def pair_lanes(fine, coarse, zf, zc):
    i, j = iota((fine, coarse), 0), iota((fine, coarse), 1)
    return ones_where(((i // zf) // 2 == j // zc) & ((i % zf) // 2 == j % zc))


def pair_lanes_back(coarse, fine, zf, zc):
    j, i = iota((coarse, fine), 0), iota((coarse, fine), 1)
    return ones_where(((i // zf) // 2 == j // zc) & ((i % zf) // 2 == j % zc))


def kernel(sizes, b_ref, ph_ref, visc_ref, mt_ref, st_ref, out_ref,
           xa0, xb0, w0, inv0, dg0, zh0, sy0, sz0, rx0, ry0, rz0,
           xa1, xb1, w1, inv1, dg1, zh1, sy1, sz1, rx1, ry1, rz1,
           s0, base0, base1, r0, r1, m1, s1, t256, t128, t64,
           pk_ms, pk_r, g_ms, g_r, x2, wj2, wj3, dj2, dj3,
           ss, rs, gsem):
    GX, GY, GZ = sizes
    N = GX * GY * GZ
    ix, iy, iz = lax.axis_index("gx"), lax.axis_index("gy"), lax.axis_index("gz")
    me = (ix * GY + iy) * GZ + iz
    axes = ((ix, GX), (iy, GY), (iz, GZ))
    L0 = dict(n=(32, 16, 128), w=w0, inv=inv0, dg=dg0, zh=zh0, sy=sy0, sz=sz0, r=(rx0, ry0, rz0), off=0, base=base0)
    L1 = dict(n=(16, 8, 64), w=w1, inv=inv1, dg=dg1, zh=zh1, sy=sy1, sz=sz1, r=(rx1, ry1, rz1), off=5, base=base1)

    def copies(L, xp, e):
        nx = L["n"][0]
        srcs = ((xp.at[1], xp.at[nx]), (L["sy"].at[0], L["sy"].at[1]), (L["sz"].at[0], L["sz"].at[1]))
        out = []
        for a in range(3):
            pos, count = axes[a]
            for side in range(2):
                to = [ix, iy, iz]
                to[a] = pos - 1 if side == 0 else pos + 1
                there = pos > 0 if side == 0 else pos < count - 1
                k = L["off"] + e
                out.append((there, pltpu.make_async_remote_copy(
                    src_ref=srcs[a][side], dst_ref=L["r"][a].at[e, 1 - side],
                    send_sem=ss.at[k, 2 * a + side], recv_sem=rs.at[k, 2 * a + 1 - side],
                    device_id=tuple(to), device_id_type=MESH), L["r"][a].at[e, side]))
        return out

    def start(L, xp, e):
        nx, ny, nz = L["n"]
        todo = copies(L, xp, e)

        def go(which):
            for there, copy, _ in which:
                @pl.when(there)
                def _(copy=copy):
                    copy.start()
        go(todo[0:2])
        for c in range(nx // CHUNK):
            v = xp[1 + c * CHUNK:1 + (c + 1) * CHUNK]
            L["sy"][0, c * CHUNK:(c + 1) * CHUNK, :] = v[:, 0, :]
            L["sy"][1, c * CHUNK:(c + 1) * CHUNK, :] = v[:, ny - 1, :]
        go(todo[2:4])
        per = LANES // ny
        for k in range(nx // per):
            t = xp[1 + k * per:1 + (k + 1) * per].reshape(LANES, LANES).T
            L["sz"][0, k:k + 1, :] = t[0:1, :]
            L["sz"][1, k:k + 1, :] = t[nz - 1:nz, :]
        go(todo[4:6])

    def finish(L, xp, e):
        nx, ny, nz = L["n"]
        todo = copies(L, xp, e)
        for a in range(3):
            for side in range(2):
                there, copy, slot = todo[2 * a + side]
                other = todo[2 * a + 1 - side][1]

                @pl.when(there)
                def _(copy=copy, other=other):
                    copy.wait_send()
                    other.wait_recv()

                @pl.when(jnp.logical_not(there))
                def _(slot=slot):
                    slot[...] = jnp.zeros(slot.shape, jnp.float32)
        rx, ry, rz = L["r"]
        xp[0] = rx[e, 0]
        xp[nx + 1] = rx[e, 1]
        per = LANES // ny
        row = iota((LANES, LANES), 0)
        for k in range(nx // per):
            low = jnp.broadcast_to(rz[e, 0, k:k + 1, :], (LANES, LANES))
            high = jnp.broadcast_to(rz[e, 1, k:k + 1, :], (LANES, LANES))
            t = jnp.where(row == 0, low, jnp.where(row == nz - 1, high, 0.0)).T
            L["zh"][k * per:(k + 1) * per] = t.reshape(per, ny, LANES)

    def around(L, xp, e, i):
        nx, ny, nz = L["n"]
        shape = (CHUNK, ny, LANES)
        ry = L["r"][1]
        at = pl.multiple_of(i * CHUNK, CHUNK)
        v = xp[pl.ds(1 + at, CHUNK)]
        zh = L["zh"][pl.ds(at, CHUNK)]
        row, lane = iota(shape, 1), iota(shape, 2)
        low = jnp.broadcast_to(ry[e, 0, pl.ds(at, CHUNK), :][:, None, :], shape)
        high = jnp.broadcast_to(ry[e, 1, pl.ds(at, CHUNK), :][:, None, :], shape)
        return v, [xp[pl.ds(2 + at, CHUNK)], xp[pl.ds(at, CHUNK)],
                   jnp.where(row == ny - 1, high, pltpu.roll(v, ny - 1, 1)),
                   jnp.where(row == 0, low, pltpu.roll(v, 1, 1)),
                   jnp.where(lane == nz - 1, zh, pltpu.roll(v, LANES - 1, 2)),
                   jnp.where(lane == 0, zh, pltpu.roll(v, 1, 2))]

    def chunks(L, fn):
        def step(i, _):
            fn(i)
            return 0
        lax.fori_loop(0, L["n"][0] // CHUNK, step, 0)

    def coefficients(L, mp, e, s_ref):
        nx, ny, nz = L["n"]

        def one(i):
            at = pl.multiple_of(i * CHUNK, CHUNK)
            m, near = around(L, mp, e, i)
            valid = iota((CHUNK, ny, LANES), 2) < nz
            diag = s_ref[pl.ds(at, CHUNK)]
            terms = []
            for n in near:
                t = 2.0 * m * n / (m + n)
                if nz < LANES:
                    t = jnp.where(valid, t, 0.0)
                diag = diag + t
                terms.append(t)
            if nz < LANES:
                diag = jnp.where(valid, diag, 1.0)
            inv = OMEGA / diag
            L["inv"][pl.ds(at, CHUNK)] = inv
            L["dg"][pl.ds(at, CHUNK)] = diag * (1.0 / OMEGA)
            for d in range(6):
                L["w"][d, pl.ds(at, CHUNK)] = terms[d] * inv
        chunks(L, one)

    def begin(L, rhs, xp):
        def one(i):
            at = pl.multiple_of(i * CHUNK, CHUNK)
            v = rhs[pl.ds(at, CHUNK)] * L["inv"][pl.ds(at, CHUNK)]
            L["base"][pl.ds(at, CHUNK)] = v
            xp[pl.ds(1 + at, CHUNK)] = v
        chunks(L, one)

    def sweep(L, xp, e, put):
        def one(i):
            at = pl.multiple_of(i * CHUNK, CHUNK)
            v, near = around(L, xp, e, i)
            total = (1.0 - OMEGA) * v + L["base"][pl.ds(at, CHUNK)]
            for d in range(6):
                total = total + L["w"][d, pl.ds(at, CHUNK)] * near[d]
            put(at, v, total)
        chunks(L, one)

    def into(xp):
        def put(at, v, total):
            xp[pl.ds(1 + at, CHUNK)] = total
        return put

    def residual(L, r):
        def put(at, v, total):
            r[pl.ds(at, CHUNK)] = L["dg"][pl.ds(at, CHUNK)] * (total - v)
        return put

    def restrict0(load):
        halve = pair_lanes(LANES, LANES, LANES, 64)
        for c in range(2):
            v = load(c).reshape(8, 2, 16, LANES)
            v = v[:, 0] + v[:, 1]
            t256[c * 128:(c + 1) * 128, :] = dot(v.reshape(128, LANES), halve)
        return (t256[pl.ds(0, 128, stride=2), :] + t256[pl.ds(1, 128, stride=2), :]).reshape(16, 8, LANES)

    def pack(v):
        v = v.reshape(8, 2, 8, LANES)
        t64[...] = (v[:, 0] + v[:, 1]).reshape(64, LANES)
        total = jnp.zeros((8, LANES), jnp.float32)
        i, j = iota((LANES, LANES), 0), iota((LANES, LANES), 1)
        for q in range(4):
            place = ones_where((i < 64) & (j == 32 * q + i // 2))
            both = t64[pl.ds(2 * q, 8, stride=8), :] + t64[pl.ds(2 * q + 1, 8, stride=8), :]
            total = total + dot(both, place)
        return total

    line = (ix * GY + iy) * GZ

    def z_peer(step):
        return (ix, iy, lax.rem(iz + step, GZ))

    def plane_peer(step):
        at = lax.rem(ix * GY + iy + step, GX * GY)
        return (at // GY, lax.rem(at, GY), iz)

    def each(count, fn):
        if count <= 8:
            for step in range(1, count):
                fn(step)
        else:
            lax.fori_loop(1, count, lambda step, _: (fn(step), 0)[1], 0)

    def greet(to):
        pl.semaphore_signal(barrier, inc=1, device_id=to, device_id_type=MESH)

    def gather_start(src, dst, k):
        def send(step):
            pltpu.make_async_remote_copy(
                src_ref=src, dst_ref=dst.at[me], send_sem=gsem.at[4 * k], recv_sem=gsem.at[4 * k + 1],
                device_id=z_peer(step), device_id_type=MESH).start()
        each(GZ, send)
        dst[pl.ds(me, 1)] = src[...][None]

    def gather_middle(src, dst, k):
        rest = dst.at[pl.ds(0, GZ - 1)]
        pltpu.make_async_copy(rest, rest, gsem.at[4 * k]).wait()
        pltpu.make_async_copy(rest, rest, gsem.at[4 * k + 1]).wait()
        lines = dst.at[pl.ds(line, GZ)]

        def send(step):
            pltpu.make_async_remote_copy(
                src_ref=lines, dst_ref=lines, send_sem=gsem.at[4 * k + 2], recv_sem=gsem.at[4 * k + 3],
                device_id=plane_peer(step), device_id_type=MESH).start()
        each(GX * GY, send)

    def gather_finish(src, dst, k):
        rest = dst.at[pl.ds(0, N - GZ)]
        pltpu.make_async_copy(rest, rest, gsem.at[4 * k + 2]).wait()
        pltpu.make_async_copy(rest, rest, gsem.at[4 * k + 3]).wait()

    X2, Y2, Z2 = 8 * GX, 4 * GY, 32 * GZ

    def unpack(read):
        lane = iota((8, LANES), 1)
        rows = []
        for gx in range(GX):
            tiles = []
            for y in range(Y2):
                gy, q = y // 4, y % 4
                for t in range(Z2 // LANES):
                    tile = jnp.zeros((8, LANES), jnp.float32)
                    for p in range(4):
                        v = read((gx * GY + gy) * GZ + 4 * t + p)
                        shift = (32 * (p - q)) % LANES
                        v = pltpu.roll(v, shift, 1) if shift else v
                        tile = jnp.where(lane // 32 == p, v, tile)
                    tiles.append(tile)
            rows.append(jnp.concatenate(tiles, axis=1))
        return jnp.concatenate(rows, axis=0)

    def flat_terms(m, s, dims):
        X, Y, Z = dims
        shape = m.shape
        row, lane = iota(shape, 0), iota(shape, 1)
        width = shape[1]
        valid = lane < Y * Z
        z, y = lane % Z, lane // Z
        inside = [row < X - 1, row > 0, y < Y - 1, y > 0, z < Z - 1, z > 0]
        diag = s
        terms = []
        for near, ok in zip(flat_near(m, Z), inside):
            t = jnp.where(ok & valid, 2.0 * m * near / (m + near), 0.0)
            diag = diag + t
            terms.append(t)
        diag = jnp.where(valid, diag, 1.0)
        inv = OMEGA / diag
        return [t * inv for t in terms], inv, diag * (1.0 / OMEGA)

    def flat_near(v, Z):
        X, width = v.shape
        return [pltpu.roll(v, X - 1, 0), pltpu.roll(v, 1, 0),
                pltpu.roll(v, width - Z, 1), pltpu.roll(v, Z, 1),
                pltpu.roll(v, width - 1, 1), pltpu.roll(v, 1, 1)]

    def flat_sweep(v, base, w, Z):
        total = (1.0 - OMEGA) * v + base
        for d, near in enumerate(flat_near(v, Z)):
            total = total + w[d] * near
        return total

    def flat_restrict(r, dims):
        X, Y, Z = dims
        span = min(4 * LANES, Y * Z)
        place = pair_lanes(span, LANES, Z, Z // 2)
        tiles = [dot(r[:, k * span:(k + 1) * span], place) for k in range(Y * Z // span)]
        wide = jnp.concatenate(tiles, axis=1) if len(tiles) > 1 else tiles[0]
        left = ones_where(iota((X // 2, X), 1) // 2 == iota((X // 2, X), 0))
        return dot(left, wide)

    def flat_spread(e, dims):
        X, Y, Z = dims
        span = min(4 * LANES, Y * Z)
        left = ones_where(iota((X, X // 2), 0) // 2 == iota((X, X // 2), 1))
        tall = dot(left, e)
        place = pair_lanes_back(LANES, span, Z, Z // 2)
        tiles = [dot(tall[:, k * LANES:(k + 1) * LANES], place) for k in range(Y * Z // span)]
        return jnp.concatenate(tiles, axis=1) if len(tiles) > 1 else tiles[0]

    d2 = (X2, Y2, Z2)
    d3 = (X2 // 2, Y2 // 2, Z2 // 2)
    d4 = (X2 // 4, Y2 // 4, Z2 // 4)

    barrier = pltpu.get_barrier_semaphore()
    each(GZ, lambda step: greet(z_peer(step)))
    each(GX * GY, lambda step: greet(plane_peer(step)))

    sz0[...] = jnp.zeros(sz0.shape, jnp.float32)
    sz1[...] = jnp.zeros(sz1.shape, jnp.float32)

    def look_up(i):
        at = pl.multiple_of(i * CHUNK, CHUNK)
        ph = ph_ref[pl.ds(at, CHUNK)]
        mob = jnp.full(ph.shape, mt_ref[0], jnp.float32)
        shift = jnp.full(ph.shape, st_ref[0], jnp.float32)
        for k in range(1, mt_ref.shape[0]):
            mob = jnp.where(ph == k, mt_ref[k], mob)
            shift = jnp.where(ph == k, st_ref[k], shift)
        xb0[pl.ds(1 + at, CHUNK)] = mob / visc_ref[pl.ds(at, CHUNK)]
        s0[pl.ds(at, CHUNK)] = shift
    chunks(L0, look_up)
    pl.semaphore_wait(barrier, GZ - 1 + GX * GY - 1)
    start(L0, xb0, 0)

    lane1 = iota((16, 8, LANES), 2)
    mob1 = restrict0(lambda c: xb0[1 + 16 * c:17 + 16 * c]) * 0.25
    xb1[1:17] = jnp.where(lane1 < 64, mob1, 1.0)
    start(L1, xb1, 0)
    s1[...] = restrict0(lambda c: s0[16 * c:16 + 16 * c])
    pk_ms[0:8, :] = pack(mob1) * 0.25
    pk_ms[8:16, :] = pack(s1[...])
    gather_start(pk_ms, g_ms, 0)

    finish(L0, xb0, 0)
    coefficients(L0, xb0, 0, s0)
    begin(L0, b_ref, xa0)
    start(L0, xa0, 1)
    finish(L1, xb1, 0)
    coefficients(L1, xb1, 0, s1)
    gather_middle(pk_ms, g_ms, 0)
    finish(L0, xa0, 1)
    sweep(L0, xa0, 1, into(xb0))
    start(L0, xb0, 2)

    gather_finish(pk_ms, g_ms, 0)
    m2 = unpack(lambda n: g_ms[n, 0:8, :])
    s2 = unpack(lambda n: g_ms[n, 8:16, :])
    w, inv, dg = flat_terms(m2, s2, d2)
    for d in range(6):
        wj2[d] = w[d]
    dj2[0], dj2[1] = inv, dg
    m3 = flat_restrict(m2, d2) * 0.25
    s3 = flat_restrict(s2, d2)
    w, inv, dg = flat_terms(m3, s3, d3)
    for d in range(6):
        wj3[d] = w[d]
    dj3[0], dj3[1] = inv, dg
    m4 = flat_restrict(m3, d3) * 0.25
    s4 = flat_restrict(s3, d3)
    w4, inv4, _ = flat_terms(m4, s4, d4)

    finish(L0, xb0, 2)
    sweep(L0, xb0, 2, residual(L0, r0))
    r1[...] = restrict0(lambda c: r0[16 * c:16 + 16 * c])
    begin(L1, r1, xa1)
    start(L1, xa1, 1)
    finish(L1, xa1, 1)
    sweep(L1, xa1, 1, into(xb1))
    start(L1, xb1, 2)
    finish(L1, xb1, 2)
    sweep(L1, xb1, 2, residual(L1, r1))
    pk_r[...] = pack(r1[...])
    gather_start(pk_r, g_r, 1)
    gather_middle(pk_r, g_r, 1)
    gather_finish(pk_r, g_r, 1)

    base2 = unpack(lambda n: g_r[n]) * dj2[0]
    w2 = [wj2.at[d] for d in range(6)]
    w3 = [wj3.at[d] for d in range(6)]

    def run(v, base, w, Z):
        return flat_sweep(v, base, [ref[...] for ref in w], Z)

    v2 = run(base2, base2, w2, Z2)
    b3 = flat_restrict(dj2[1] * (run(v2, base2, w2, Z2) - v2), d2)
    base3 = b3 * dj3[0]
    v3 = run(base3, base3, w3, Z2 // 2)
    b4 = flat_restrict(dj3[1] * (run(v3, base3, w3, Z2 // 2) - v3), d3)
    base4 = b4 * inv4
    v4 = lax.fori_loop(0, COARSE_SWEEPS - 1, lambda _, v: flat_sweep(v, base4, w4, Z2 // 4), base4)
    v3 = v3 + flat_spread(v4, d3)
    for _ in range(2):
        v3 = run(v3, base3, w3, Z2 // 2)
    v2 = v2 + flat_spread(v3, d2)
    for _ in range(2):
        v2 = run(v2, base2, w2, Z2)
    x2[...] = v2

    widen32 = ones_where((iota((LANES, LANES), 1) // 2 == iota((LANES, LANES), 0)) & (iota((LANES, LANES), 1) < 64))
    for q in range(4):
        column = pl.multiple_of((iy * 4 + q) * Z2 + (iz // 4) * LANES, LANES)
        tile = x2[pl.ds(pl.multiple_of(ix * 8, 8), 8), pl.ds(column, LANES)]
        tile = pltpu.roll(tile, lax.rem(LANES - 32 * lax.rem(iz, 4), LANES), 1)
        tile = dot(tile, widen32)
        t64[pl.ds(2 * q, 8, stride=8), :] = tile
        t64[pl.ds(2 * q + 1, 8, stride=8), :] = tile
    e1 = jnp.broadcast_to(t64[...].reshape(8, 1, 8, LANES), (8, 2, 8, LANES)).reshape(16, 8, LANES)
    xa1[1:17] = xb1[1:17] + e1
    start(L1, xa1, 3)
    finish(L1, xa1, 3)
    sweep(L1, xa1, 3, into(xb1))
    start(L1, xb1, 4)
    finish(L1, xb1, 4)
    sweep(L1, xb1, 4, into(xa1))

    widen64 = pair_lanes_back(LANES, LANES, LANES, 64)
    wide = dot(xa1[1:17].reshape(128, LANES), widen64)
    t256[pl.ds(0, 128, stride=2), :] = wide
    t256[pl.ds(1, 128, stride=2), :] = wide
    for c in range(16):
        e0 = t256[16 * c:16 * c + 16, :]
        xa0[1 + 2 * c] = xb0[1 + 2 * c] + e0
        xa0[2 + 2 * c] = xb0[2 + 2 * c] + e0
    start(L0, xa0, 3)
    finish(L0, xa0, 3)
    sweep(L0, xa0, 3, into(xb0))
    start(L0, xb0, 4)
    finish(L0, xb0, 4)

    def put(at, v, total):
        out_ref[pl.ds(at, CHUNK)] = total
    sweep(L0, xb0, 4, put)


def body(sizes, right_side, phase_label, viscosity, mobility_table, shift_table):
    GX, GY, GZ = sizes
    N = GX * GY * GZ
    f32 = jnp.float32
    V = lambda *shape: pltpu.VMEM(shape, f32)

    def level(nx, ny):
        return [V(nx + 2, ny, 128), V(nx + 2, ny, 128), V(6, nx, ny, 128), V(nx, ny, 128), V(nx, ny, 128), V(nx, ny, 128),
                V(2, nx, 128), V(2, 8, 128), V(5, 2, ny, 128), V(5, 2, nx, 128), V(5, 2, 8, 128)]

    X2, F2 = 8 * GX, 128 * GY * GZ
    X3, F3 = 4 * GX, max(128, 32 * GY * GZ)
    scratch = level(32, 16) + level(16, 8) + [
        V(32, 16, 128), V(32, 16, 128), V(16, 8, 128), V(32, 16, 128), V(16, 8, 128), V(16, 8, 128), V(16, 8, 128),
        V(256, 128), V(128, 128), V(64, 128),
        V(16, 128), V(8, 128), V(N, 16, 128), V(N, 8, 128),
        V(X2, F2), V(6, X2, F2), V(6, X3, F3), V(2, X2, F2), V(2, X3, F3),
        pltpu.SemaphoreType.DMA((10, 6)), pltpu.SemaphoreType.DMA((10, 6)), pltpu.SemaphoreType.DMA((8,))]
    vmem = pl.BlockSpec(memory_space=pltpu.VMEM)
    smem = pl.BlockSpec(memory_space=pltpu.SMEM)
    return pl.pallas_call(
        functools.partial(kernel, sizes),
        out_shape=jax.ShapeDtypeStruct(right_side.shape, f32),
        in_specs=[vmem, vmem, vmem, smem, smem],
        out_specs=vmem,
        scratch_shapes=scratch,
        compiler_params=pltpu.CompilerParams(has_side_effects=True, collective_id=0, vmem_limit_bytes=56 * 2**20),
    )(right_side, phase_label, viscosity, mobility_table, shift_table)


def solution(mesh):
    sizes = tuple(mesh.shape[a] for a in ("gx", "gy", "gz"))
    in_specs = (P("gx", "gy", "gz"), P("gx", "gy", "gz"), P("gx", "gy", "gz"), P(), P())
    return jax.shard_map(functools.partial(body, sizes), mesh=mesh, in_specs=in_specs,
                         out_specs=P("gx", "gy", "gz"), check_vma=False)
```

```python
import functools
import jax
import jax.numpy as jnp
from jax import lax
from jax.sharding import PartitionSpec as P
from jax.experimental import pallas as pl
from jax.experimental.pallas import tpu as pltpu

LEVELS = 5
COARSE_SWEEPS = 48
OMEGA = 0.8
LANES = 128
CHUNK = 8
MESH = pl.DeviceIdType.MESH


def parts(v):
    high = v.astype(jnp.bfloat16)
    left = v - high.astype(jnp.float32)
    middle = left.astype(jnp.bfloat16)
    low = (left - middle.astype(jnp.float32)).astype(jnp.bfloat16)
    return high, middle, low


def dot(a, place):
    place = place.astype(jnp.bfloat16)
    high, middle, low = [jnp.dot(p, place, preferred_element_type=jnp.float32) for p in parts(a)]
    return high + (middle + low)


def left_dot(place, b):
    place = place.astype(jnp.bfloat16)
    high, middle, low = [jnp.dot(place, p, preferred_element_type=jnp.float32) for p in parts(b)]
    return high + (middle + low)


def iota(shape, dim):
    return lax.broadcasted_iota(jnp.int32, shape, dim)


def ones_where(mask):
    return jnp.where(mask, 1.0, 0.0).astype(jnp.float32)


def over(i, n):
    return i >> (n.bit_length() - 1) if n & (n - 1) == 0 else i // n


def rest(i, n):
    return i & (n - 1) if n & (n - 1) == 0 else i % n


def pair_lanes(fine, coarse, zf, zc):
    i, j = iota((fine, coarse), 0), iota((fine, coarse), 1)
    return ones_where(((over(i, zf) >> 1) == over(j, zc)) & ((rest(i, zf) >> 1) == rest(j, zc)))


def pair_lanes_back(coarse, fine, zf, zc):
    j, i = iota((coarse, fine), 0), iota((coarse, fine), 1)
    return ones_where(((over(i, zf) >> 1) == over(j, zc)) & ((rest(i, zf) >> 1) == rest(j, zc)))


def kernel(sizes, b_ref, ph_ref, visc_ref, mt_ref, st_ref, out_ref,
           xa0, xb0, w0, inv0, dg0, zh0, sy0, sz0, rx0, ry0, rz0,
           xa1, xb1, w1, inv1, dg1, zh1, sy1, sz1, rx1, ry1, rz1,
           s0, base0, base1, r0, r1, m1, s1, t256, t128, t64,
           pk_ms, pk_r, g_ms, g_r, x2, wj2, wj3, dj2, dj3,
           ss, rs, gsem):
    GX, GY, GZ = sizes
    N = GX * GY * GZ
    ix, iy, iz = lax.axis_index("gx"), lax.axis_index("gy"), lax.axis_index("gz")
    me = (ix * GY + iy) * GZ + iz
    axes = ((ix, GX), (iy, GY), (iz, GZ))
    L0 = dict(n=(32, 16, 128), w=w0, inv=inv0, dg=dg0, zh=zh0, sy=sy0, sz=sz0, r=(rx0, ry0, rz0), off=0, base=base0)
    L1 = dict(n=(16, 8, 64), w=w1, inv=inv1, dg=dg1, zh=zh1, sy=sy1, sz=sz1, r=(rx1, ry1, rz1), off=5, base=base1)

    def copies(L, xp, e):
        nx = L["n"][0]
        srcs = ((xp.at[1], xp.at[nx]), (L["sy"].at[0], L["sy"].at[1]), (L["sz"].at[0], L["sz"].at[1]))
        out = []
        for a in range(3):
            pos, count = axes[a]
            for side in range(2):
                to = [ix, iy, iz]
                to[a] = pos - 1 if side == 0 else pos + 1
                there = pos > 0 if side == 0 else pos < count - 1
                k = L["off"] + e
                out.append((there, pltpu.make_async_remote_copy(
                    src_ref=srcs[a][side], dst_ref=L["r"][a].at[e, 1 - side],
                    send_sem=ss.at[k, 2 * a + side], recv_sem=rs.at[k, 2 * a + 1 - side],
                    device_id=tuple(to), device_id_type=MESH), L["r"][a].at[e, side]))
        return out

    def start(L, xp, e):
        nx, ny, nz = L["n"]
        todo = copies(L, xp, e)

        def go(which):
            for there, copy, _ in which:
                @pl.when(there)
                def _(copy=copy):
                    copy.start()
        go(todo[0:2])
        for c in range(nx // CHUNK):
            v = xp[1 + c * CHUNK:1 + (c + 1) * CHUNK]
            L["sy"][0, c * CHUNK:(c + 1) * CHUNK, :] = v[:, 0, :]
            L["sy"][1, c * CHUNK:(c + 1) * CHUNK, :] = v[:, ny - 1, :]
        go(todo[2:4])
        per = LANES // ny
        for k in range(nx // per):
            t = xp[1 + k * per:1 + (k + 1) * per].reshape(LANES, LANES).T
            L["sz"][0, k:k + 1, :] = t[0:1, :]
            L["sz"][1, k:k + 1, :] = t[nz - 1:nz, :]
        go(todo[4:6])

    def finish(L, xp, e):
        nx, ny, nz = L["n"]
        todo = copies(L, xp, e)
        for a in range(3):
            for side in range(2):
                there, copy, slot = todo[2 * a + side]
                other = todo[2 * a + 1 - side][1]

                @pl.when(there)
                def _(copy=copy, other=other):
                    copy.wait_send()
                    other.wait_recv()

                @pl.when(jnp.logical_not(there))
                def _(slot=slot):
                    slot[...] = jnp.zeros(slot.shape, jnp.float32)
        rx, ry, rz = L["r"]
        xp[0] = rx[e, 0]
        xp[nx + 1] = rx[e, 1]
        per = LANES // ny
        row = iota((LANES, LANES), 0)
        for k in range(nx // per):
            low = jnp.broadcast_to(rz[e, 0, k:k + 1, :], (LANES, LANES))
            high = jnp.broadcast_to(rz[e, 1, k:k + 1, :], (LANES, LANES))
            t = jnp.where(row == 0, low, jnp.where(row == nz - 1, high, 0.0)).T
            L["zh"][k * per:(k + 1) * per] = t.reshape(per, ny, LANES)

    def around(L, xp, e, i):
        nx, ny, nz = L["n"]
        shape = (CHUNK, ny, LANES)
        ry = L["r"][1]
        at = pl.multiple_of(i * CHUNK, CHUNK)
        v = xp[pl.ds(1 + at, CHUNK)]
        zh = L["zh"][pl.ds(at, CHUNK)]
        row, lane = iota(shape, 1), iota(shape, 2)
        low = jnp.broadcast_to(ry[e, 0, pl.ds(at, CHUNK), :][:, None, :], shape)
        high = jnp.broadcast_to(ry[e, 1, pl.ds(at, CHUNK), :][:, None, :], shape)
        return v, [xp[pl.ds(2 + at, CHUNK)], xp[pl.ds(at, CHUNK)],
                   jnp.where(row == ny - 1, high, pltpu.roll(v, ny - 1, 1)),
                   jnp.where(row == 0, low, pltpu.roll(v, 1, 1)),
                   jnp.where(lane == nz - 1, zh, pltpu.roll(v, LANES - 1, 2)),
                   jnp.where(lane == 0, zh, pltpu.roll(v, 1, 2))]

    def chunks(L, fn):
        def step(i, _):
            fn(i)
            return 0
        lax.fori_loop(0, L["n"][0] // CHUNK, step, 0)

    def coefficients(L, mp, e, s_ref):
        nx, ny, nz = L["n"]

        def one(i):
            at = pl.multiple_of(i * CHUNK, CHUNK)
            m, near = around(L, mp, e, i)
            valid = iota((CHUNK, ny, LANES), 2) < nz
            diag = s_ref[pl.ds(at, CHUNK)]
            terms = []
            for n in near:
                t = 2.0 * m * n / (m + n)
                if nz < LANES:
                    t = jnp.where(valid, t, 0.0)
                diag = diag + t
                terms.append(t)
            if nz < LANES:
                diag = jnp.where(valid, diag, 1.0)
            inv = OMEGA / diag
            L["inv"][pl.ds(at, CHUNK)] = inv
            L["dg"][pl.ds(at, CHUNK)] = diag * (1.0 / OMEGA)
            for d in range(6):
                L["w"][d, pl.ds(at, CHUNK)] = terms[d] * inv
        chunks(L, one)

    def begin(L, rhs, xp):
        def one(i):
            at = pl.multiple_of(i * CHUNK, CHUNK)
            v = rhs[pl.ds(at, CHUNK)] * L["inv"][pl.ds(at, CHUNK)]
            L["base"][pl.ds(at, CHUNK)] = v
            xp[pl.ds(1 + at, CHUNK)] = v
        chunks(L, one)

    def sweep(L, xp, e, put):
        def one(i):
            at = pl.multiple_of(i * CHUNK, CHUNK)
            v, near = around(L, xp, e, i)
            total = (1.0 - OMEGA) * v + L["base"][pl.ds(at, CHUNK)]
            for d in range(6):
                total = total + L["w"][d, pl.ds(at, CHUNK)] * near[d]
            put(at, v, total)
        chunks(L, one)

    def into(xp):
        def put(at, v, total):
            xp[pl.ds(1 + at, CHUNK)] = total
        return put

    def residual(L, r):
        def put(at, v, total):
            r[pl.ds(at, CHUNK)] = L["dg"][pl.ds(at, CHUNK)] * (total - v)
        return put

    def restrict0(load):
        halve = pair_lanes(LANES, LANES, LANES, 64)
        for c in range(2):
            v = load(c).reshape(8, 2, 16, LANES)
            v = v[:, 0] + v[:, 1]
            t256[c * 128:(c + 1) * 128, :] = dot(v.reshape(128, LANES), halve)
        return (t256[pl.ds(0, 128, stride=2), :] + t256[pl.ds(1, 128, stride=2), :]).reshape(16, 8, LANES)

    def pack(v):
        v = v.reshape(8, 2, 8, LANES)
        t64[...] = (v[:, 0] + v[:, 1]).reshape(64, LANES)
        total = jnp.zeros((8, LANES), jnp.float32)
        i, j = iota((LANES, LANES), 0), iota((LANES, LANES), 1)
        for q in range(4):
            place = ones_where((i < 64) & (j == 32 * q + i // 2))
            both = t64[pl.ds(2 * q, 8, stride=8), :] + t64[pl.ds(2 * q + 1, 8, stride=8), :]
            total = total + dot(both, place)
        return total

    line = (ix * GY + iy) * GZ

    def z_peer(step):
        return (ix, iy, lax.rem(iz + step, GZ))

    def plane_peer(step):
        at = lax.rem(ix * GY + iy + step, GX * GY)
        return (at // GY, lax.rem(at, GY), iz)

    def each(count, fn):
        if count <= 8:
            for step in range(1, count):
                fn(step)
        else:
            lax.fori_loop(1, count, lambda step, _: (fn(step), 0)[1], 0)

    def greet(to):
        pl.semaphore_signal(barrier, inc=1, device_id=to, device_id_type=MESH)

    def gather_start(src, dst, k):
        def send(step):
            pltpu.make_async_remote_copy(
                src_ref=src, dst_ref=dst.at[me], send_sem=gsem.at[4 * k], recv_sem=gsem.at[4 * k + 1],
                device_id=z_peer(step), device_id_type=MESH).start()
        each(GZ, send)
        dst[pl.ds(me, 1)] = src[...][None]

    def gather_middle(src, dst, k):
        part = dst.at[pl.ds(0, GZ - 1)]
        pltpu.make_async_copy(part, part, gsem.at[4 * k]).wait()
        pltpu.make_async_copy(part, part, gsem.at[4 * k + 1]).wait()
        lines = dst.at[pl.ds(line, GZ)]

        def send(step):
            pltpu.make_async_remote_copy(
                src_ref=lines, dst_ref=lines, send_sem=gsem.at[4 * k + 2], recv_sem=gsem.at[4 * k + 3],
                device_id=plane_peer(step), device_id_type=MESH).start()
        each(GX * GY, send)

    def gather_finish(src, dst, k):
        part = dst.at[pl.ds(0, N - GZ)]
        pltpu.make_async_copy(part, part, gsem.at[4 * k + 2]).wait()
        pltpu.make_async_copy(part, part, gsem.at[4 * k + 3]).wait()

    X2, Y2, Z2 = 8 * GX, 4 * GY, 32 * GZ

    def unpack(read):
        lane = iota((8, LANES), 1)
        rows = []
        for gx in range(GX):
            tiles = []
            for y in range(Y2):
                gy, q = y // 4, y % 4
                for t in range(Z2 // LANES):
                    tile = jnp.zeros((8, LANES), jnp.float32)
                    for p in range(4):
                        v = read((gx * GY + gy) * GZ + 4 * t + p)
                        shift = (32 * (p - q)) % LANES
                        v = pltpu.roll(v, shift, 1) if shift else v
                        tile = jnp.where((lane >> 5) == p, v, tile)
                    tiles.append(tile)
            rows.append(jnp.concatenate(tiles, axis=1))
        return jnp.concatenate(rows, axis=0)

    def flat_terms(m, s, dims):
        X, Y, Z = dims
        shape = m.shape
        row, lane = iota(shape, 0), iota(shape, 1)
        width = shape[1]
        valid = lane < Y * Z
        z, y = rest(lane, Z), over(lane, Z)
        inside = [row < X - 1, row > 0, y < Y - 1, y > 0, z < Z - 1, z > 0]
        diag = s
        terms = []
        for near, ok in zip(flat_near(m, Z), inside):
            t = jnp.where(ok & valid, 2.0 * m * near / (m + near), 0.0)
            diag = diag + t
            terms.append(t)
        diag = jnp.where(valid, diag, 1.0)
        inv = OMEGA / diag
        return [t * inv for t in terms], inv, diag * (1.0 / OMEGA)

    def flat_near(v, Z):
        X, width = v.shape
        return [pltpu.roll(v, X - 1, 0), pltpu.roll(v, 1, 0),
                pltpu.roll(v, width - Z, 1), pltpu.roll(v, Z, 1),
                pltpu.roll(v, width - 1, 1), pltpu.roll(v, 1, 1)]

    def flat_sweep(v, base, w, Z):
        total = (1.0 - OMEGA) * v + base
        for d, near in enumerate(flat_near(v, Z)):
            total = total + w[d] * near
        return total

    def flat_restrict(r, dims):
        X, Y, Z = dims
        span = min(4 * LANES, Y * Z)
        place = pair_lanes(span, LANES, Z, Z // 2)
        tiles = [dot(r[:, k * span:(k + 1) * span], place) for k in range(Y * Z // span)]
        wide = jnp.concatenate(tiles, axis=1) if len(tiles) > 1 else tiles[0]
        left = ones_where(iota((X // 2, X), 1) // 2 == iota((X // 2, X), 0))
        return left_dot(left, wide)

    def flat_spread(e, dims):
        X, Y, Z = dims
        span = min(4 * LANES, Y * Z)
        left = ones_where(iota((X, X // 2), 0) // 2 == iota((X, X // 2), 1))
        tall = left_dot(left, e)
        place = pair_lanes_back(LANES, span, Z, Z // 2)
        tiles = [dot(tall[:, k * LANES:(k + 1) * LANES], place) for k in range(Y * Z // span)]
        return jnp.concatenate(tiles, axis=1) if len(tiles) > 1 else tiles[0]

    d2 = (X2, Y2, Z2)
    d3 = (X2 // 2, Y2 // 2, Z2 // 2)
    d4 = (X2 // 4, Y2 // 4, Z2 // 4)

    barrier = pltpu.get_barrier_semaphore()
    each(GZ, lambda step: greet(z_peer(step)))
    each(GX * GY, lambda step: greet(plane_peer(step)))

    sz0[...] = jnp.zeros(sz0.shape, jnp.float32)
    sz1[...] = jnp.zeros(sz1.shape, jnp.float32)

    def look_up(i):
        at = pl.multiple_of(i * CHUNK, CHUNK)
        ph = ph_ref[pl.ds(at, CHUNK)]
        mob = jnp.full(ph.shape, mt_ref[0], jnp.float32)
        shift = jnp.full(ph.shape, st_ref[0], jnp.float32)
        for k in range(1, mt_ref.shape[0]):
            mob = jnp.where(ph == k, mt_ref[k], mob)
            shift = jnp.where(ph == k, st_ref[k], shift)
        xb0[pl.ds(1 + at, CHUNK)] = mob / visc_ref[pl.ds(at, CHUNK)]
        s0[pl.ds(at, CHUNK)] = shift
    chunks(L0, look_up)
    pl.semaphore_wait(barrier, GZ - 1 + GX * GY - 1)
    start(L0, xb0, 0)

    lane1 = iota((16, 8, LANES), 2)
    mob1 = restrict0(lambda c: xb0[1 + 16 * c:17 + 16 * c]) * 0.25
    xb1[1:17] = jnp.where(lane1 < 64, mob1, 1.0)
    start(L1, xb1, 0)
    s1[...] = restrict0(lambda c: s0[16 * c:16 + 16 * c])
    pk_ms[0:8, :] = pack(mob1) * 0.25
    pk_ms[8:16, :] = pack(s1[...])
    gather_start(pk_ms, g_ms, 0)

    finish(L0, xb0, 0)
    coefficients(L0, xb0, 0, s0)
    begin(L0, b_ref, xa0)
    start(L0, xa0, 1)
    finish(L1, xb1, 0)
    coefficients(L1, xb1, 0, s1)
    gather_middle(pk_ms, g_ms, 0)
    finish(L0, xa0, 1)
    sweep(L0, xa0, 1, into(xb0))
    start(L0, xb0, 2)

    gather_finish(pk_ms, g_ms, 0)
    m2 = unpack(lambda n: g_ms[n, 0:8, :])
    s2 = unpack(lambda n: g_ms[n, 8:16, :])
    w, inv, dg = flat_terms(m2, s2, d2)
    for d in range(6):
        wj2[d] = w[d]
    dj2[0], dj2[1] = inv, dg
    m3 = flat_restrict(m2, d2) * 0.25
    s3 = flat_restrict(s2, d2)

    finish(L0, xb0, 2)
    sweep(L0, xb0, 2, residual(L0, r0))
    r1[...] = restrict0(lambda c: r0[16 * c:16 + 16 * c])
    begin(L1, r1, xa1)
    start(L1, xa1, 1)
    w, inv, dg = flat_terms(m3, s3, d3)
    for d in range(6):
        wj3[d] = w[d]
    dj3[0], dj3[1] = inv, dg
    m4 = flat_restrict(m3, d3) * 0.25
    s4 = flat_restrict(s3, d3)
    finish(L1, xa1, 1)
    sweep(L1, xa1, 1, into(xb1))
    start(L1, xb1, 2)
    w4, inv4, _ = flat_terms(m4, s4, d4)
    finish(L1, xb1, 2)
    sweep(L1, xb1, 2, residual(L1, r1))
    pk_r[...] = pack(r1[...])
    gather_start(pk_r, g_r, 1)
    gather_middle(pk_r, g_r, 1)
    gather_finish(pk_r, g_r, 1)

    base2 = unpack(lambda n: g_r[n]) * dj2[0]
    w2 = [wj2.at[d] for d in range(6)]
    w3 = [wj3.at[d] for d in range(6)]

    def run(v, base, w, Z):
        return flat_sweep(v, base, [ref[...] for ref in w], Z)

    v2 = run(base2, base2, w2, Z2)
    b3 = flat_restrict(dj2[1] * (run(v2, base2, w2, Z2) - v2), d2)
    base3 = b3 * dj3[0]
    v3 = run(base3, base3, w3, Z2 // 2)
    b4 = flat_restrict(dj3[1] * (run(v3, base3, w3, Z2 // 2) - v3), d3)
    base4 = b4 * inv4
    v4 = lax.fori_loop(0, COARSE_SWEEPS - 1, lambda _, v: flat_sweep(v, base4, w4, Z2 // 4), base4)
    v3 = v3 + flat_spread(v4, d3)
    for _ in range(2):
        v3 = run(v3, base3, w3, Z2 // 2)
    v2 = v2 + flat_spread(v3, d2)
    for _ in range(2):
        v2 = run(v2, base2, w2, Z2)
    x2[...] = v2

    widen32 = ones_where((iota((LANES, LANES), 1) // 2 == iota((LANES, LANES), 0)) & (iota((LANES, LANES), 1) < 64))
    for q in range(4):
        column = pl.multiple_of((iy * 4 + q) * Z2 + (iz // 4) * LANES, LANES)
        tile = x2[pl.ds(pl.multiple_of(ix * 8, 8), 8), pl.ds(column, LANES)]
        tile = pltpu.roll(tile, lax.rem(LANES - 32 * lax.rem(iz, 4), LANES), 1)
        tile = dot(tile, widen32)
        t64[pl.ds(2 * q, 8, stride=8), :] = tile
        t64[pl.ds(2 * q + 1, 8, stride=8), :] = tile
    e1 = jnp.broadcast_to(t64[...].reshape(8, 1, 8, LANES), (8, 2, 8, LANES)).reshape(16, 8, LANES)
    xa1[1:17] = xb1[1:17] + e1
    start(L1, xa1, 3)
    finish(L1, xa1, 3)
    sweep(L1, xa1, 3, into(xb1))
    start(L1, xb1, 4)
    finish(L1, xb1, 4)
    sweep(L1, xb1, 4, into(xa1))

    widen64 = pair_lanes_back(LANES, LANES, LANES, 64)
    wide = dot(xa1[1:17].reshape(128, LANES), widen64)
    t256[pl.ds(0, 128, stride=2), :] = wide
    t256[pl.ds(1, 128, stride=2), :] = wide
    for c in range(16):
        e0 = t256[16 * c:16 * c + 16, :]
        xa0[1 + 2 * c] = xb0[1 + 2 * c] + e0
        xa0[2 + 2 * c] = xb0[2 + 2 * c] + e0
    start(L0, xa0, 3)
    finish(L0, xa0, 3)
    sweep(L0, xa0, 3, into(xb0))
    start(L0, xb0, 4)
    finish(L0, xb0, 4)

    def put(at, v, total):
        out_ref[pl.ds(at, CHUNK)] = total
    sweep(L0, xb0, 4, put)


def body(sizes, right_side, phase_label, viscosity, mobility_table, shift_table):
    GX, GY, GZ = sizes
    N = GX * GY * GZ
    f32 = jnp.float32
    V = lambda *shape: pltpu.VMEM(shape, f32)

    def level(nx, ny):
        return [V(nx + 2, ny, 128), V(nx + 2, ny, 128), V(6, nx, ny, 128), V(nx, ny, 128), V(nx, ny, 128), V(nx, ny, 128),
                V(2, nx, 128), V(2, 8, 128), V(5, 2, ny, 128), V(5, 2, nx, 128), V(5, 2, 8, 128)]

    X2, F2 = 8 * GX, 128 * GY * GZ
    X3, F3 = 4 * GX, max(128, 32 * GY * GZ)
    scratch = level(32, 16) + level(16, 8) + [
        V(32, 16, 128), V(32, 16, 128), V(16, 8, 128), V(32, 16, 128), V(16, 8, 128), V(16, 8, 128), V(16, 8, 128),
        V(256, 128), V(128, 128), V(64, 128),
        V(16, 128), V(8, 128), V(N, 16, 128), V(N, 8, 128),
        V(X2, F2), V(6, X2, F2), V(6, X3, F3), V(2, X2, F2), V(2, X3, F3),
        pltpu.SemaphoreType.DMA((10, 6)), pltpu.SemaphoreType.DMA((10, 6)), pltpu.SemaphoreType.DMA((8,))]
    vmem = pl.BlockSpec(memory_space=pltpu.VMEM)
    smem = pl.BlockSpec(memory_space=pltpu.SMEM)
    return pl.pallas_call(
        functools.partial(kernel, sizes),
        out_shape=jax.ShapeDtypeStruct(right_side.shape, f32),
        in_specs=[vmem, vmem, vmem, smem, smem],
        out_specs=vmem,
        scratch_shapes=scratch,
        compiler_params=pltpu.CompilerParams(has_side_effects=True, collective_id=0, vmem_limit_bytes=56 * 2**20),
    )(right_side, phase_label, viscosity, mobility_table, shift_table)


def solution(mesh):
    sizes = tuple(mesh.shape[a] for a in ("gx", "gy", "gz"))
    in_specs = (P("gx", "gy", "gz"), P("gx", "gy", "gz"), P("gx", "gy", "gz"), P(), P())
    return jax.shard_map(functools.partial(body, sizes), mesh=mesh, in_specs=in_specs,
                         out_specs=P("gx", "gy", "gz"), check_vma=False)
```
